768 devices in a mesh: sx: 48 (over y, z_lo), sy: 16 (over z_hi, x, core).
Axes of the slice: x: 4, y: 8, z: 12 (z_hi: 2, z_lo: 6; z = z_hi * 6 + z_lo), core: 2. Of those that a mesh axis runs over, the one named last changes fastest.
Arguments:
- schur: bfloat16 [48, 4096, 4096], P('sx', 'sy'), as said below
- precond: bfloat16 [48, 4096, 4096], P('sx', 'sy'), as said below
- right_side: float32 [48, 32, 2048], P('sx', None, 'sy')
- matching: int32 [48, 2048], P('sx', 'sy'), may hold values from 0 to 127, as said below
Outputs:
- solution: float32 [48, 32, 2048], P('sx', None, 'sy')
- residual: float32 [48, 32, 2048], P('sx', None, 'sy')
The draws below stay inside these ranges and needn't reach their ends.
Inputs may be any that keep to these rules, and one draw needn't show every extreme that they name: `schur`: each subdomain's matrix is symmetric positive definite. `precond`: each subdomain's matrix is symmetric positive definite. `matching`: each aligned block of 128 entries of a row is a permutation of 0 to 127.
All inputs are finite; a program needn't handle non-finite values.
Results may differ from the reference program's by a relative error of at most 0.007.
The reference program's roundings to bfloat16 on the way count: a program that leaves them out, or rounds other values in their place, can miss the bound.
Values may be sent and summed in bfloat16 or wider, within the bound.
A program may use at most 32 MiB of HBM per device.

```python
import math
import jax
import jax.numpy as jnp
from jax import lax

NLOC = 4096
K = 32
ITERS = 2
NSUB = 48
FACE = 2048
FB = 128


def spd_blocks(key, low, high, factor):
    keys = jax.random.split(jax.random.fold_in(key, 11), NSUB)
    dkey = jax.random.fold_in(key, 23)
    diag_rows = low * jnp.exp(math.log(high / low) * jax.random.uniform(dkey, (NSUB, NLOC), jnp.float32))
    rows = lax.broadcasted_iota(jnp.int32, (NLOC, NLOC), 0)
    cols = lax.broadcasted_iota(jnp.int32, (NLOC, NLOC), 1)

    def one(pair):
        sub_key, diag_one = pair
        entries = jnp.clip(jax.random.normal(sub_key, (NLOC, NLOC), jnp.float32), -3.0, 3.0)
        coupled = (entries + entries.T) * (factor / math.sqrt(NLOC))
        return jnp.where(rows == cols, diag_one[:, None], coupled).astype(jnp.bfloat16)
    return lax.map(one, (keys, diag_rows))


def draw_schur(key, part):
    return spd_blocks(jax.random.fold_in(key, 101), 1.0, 2.0, 0.25)


def draw_precond(key, part):
    return spd_blocks(jax.random.fold_in(key, 202), 0.6, 1.2, 0.12)


def draw_right_side(key, part):
    sub = lax.broadcasted_iota(jnp.float32, (NSUB, 1, 1), 0) / max(NSUB - 1, 1)
    pos = lax.broadcasted_iota(jnp.float32, (1, 1, FACE), 2) / max(FACE - 1, 1)
    ramp = jnp.power(3.0, sub) * jnp.power(3.0, pos)
    k1 = jax.random.fold_in(jax.random.fold_in(key, 303), 0)
    return jax.random.normal(k1, (NSUB, K, FACE), jnp.float32) * ramp


def draw_matching(key, part):
    keys = jax.random.split(jax.random.fold_in(key, 404), NSUB * (FACE // FB))
    perms = jax.vmap(lambda one_key: jax.random.permutation(one_key, FB))(keys)
    return perms.reshape(NSUB, FACE).astype(jnp.int32)


def setup_inputs(seed: int = 0) -> dict:
    key_of = jax.random.split(jax.random.key(seed), 5)
    schur = draw_schur(jax.random.fold_in(key_of[4], 71), 0)
    precond = draw_precond(jax.random.fold_in(key_of[4], 71), 0)
    right_side = draw_right_side(jax.random.fold_in(key_of[4], 71), 0)
    matching = draw_matching(jax.random.fold_in(key_of[4], 71), 0)
    return {"schur": schur, "precond": precond, "right_side": right_side, "matching": matching}


def face_maps(matching):
    offsets = lax.broadcasted_iota(jnp.int32, matching.shape, 1) // FB * FB
    gidx = (matching + offsets).astype(jnp.int32)
    inverse = jnp.argsort(gidx, axis=1).astype(jnp.int32)
    return (gidx, inverse)

def apply_op(matrix, block, gidx, inverse):
    taken = jnp.take_along_axis(block, gidx[:, None, :], axis=2)
    right_part = jnp.roll(taken, -1, axis=0)
    nblocks = FACE // FB
    left_view = block.reshape(NSUB, K, nblocks, FB)
    right_view = right_part.reshape(NSUB, K, nblocks, FB)
    local = jnp.concatenate([left_view, right_view], axis=3).reshape(NSUB, K, NLOC)

    def one(pair):
        mat, vec = pair
        return jnp.dot(vec.astype(jnp.float32), mat.T.astype(jnp.float32), preferred_element_type=jnp.float32)
    prod = lax.map(one, (matrix, local)).reshape(NSUB, K, nblocks, 2 * FB)
    left_out = prod[:, :, :, :FB].reshape(NSUB, K, FACE)
    right_out = prod[:, :, :, FB:].reshape(NSUB, K, FACE)
    came = jnp.roll(right_out, 1, axis=0)
    return left_out + jnp.take_along_axis(came, inverse[:, None, :], axis=2)

def gram(first, second):
    total = jnp.einsum('jkf,jlf->kl', first, second, precision=lax.Precision.HIGHEST)
    return 0.5 * (total + total.T)

def solve_spd(matrix, rhs):
    lower = jnp.linalg.cholesky(matrix)
    return jax.scipy.linalg.cho_solve((lower, True), rhs)

def combine(coeff, block):
    return jnp.einsum('kl,jkf->jlf', coeff, block, precision=lax.Precision.HIGHEST)

def reference(schur, precond, right_side, matching):
    gidx, inverse = face_maps(matching)
    residual = right_side
    solution = jnp.zeros_like(right_side)
    search = apply_op(precond, residual.astype(jnp.bfloat16), gidx, inverse)
    gamma = gram(residual, search)
    for step in range(ITERS):
        image = apply_op(schur, search.astype(jnp.bfloat16), gidx, inverse)
        delta = gram(search, image)
        alpha = solve_spd(delta, gamma)
        solution = solution + combine(alpha, search)
        residual = residual - combine(alpha, image)
        if step + 1 < ITERS:
            precd = apply_op(precond, residual.astype(jnp.bfloat16), gidx, inverse)
            gnew = gram(residual, precd)
            beta = solve_spd(gamma, gnew)
            search = precd + combine(beta, search)
            gamma = gnew
    return (solution, residual)
```

```python
import functools

import jax
import jax.numpy as jnp
from jax import lax
from jax.experimental import pallas as pl
from jax.experimental.pallas import tpu as pltpu
from jax.sharding import PartitionSpec as P

F32, BF16 = jnp.float32, jnp.bfloat16
MESH = pl.DeviceIdType.MESH
NY, NZL, NZH, NXC = 8, 6, 2, 8
NZ = NZL * NZH
K, FB = 32, 128


def split3(value):
    high = value.astype(BF16)
    rest = value - high.astype(F32)
    middle = rest.astype(BF16)
    low = (rest - middle.astype(F32)).astype(BF16)
    return high, middle, low


def moved(value, onehot, dim):
    parts = jnp.concatenate(split3(value), axis=0)
    out = lax.dot_general(parts, onehot, (((1,), (dim,)), ((), ())), preferred_element_type=F32)
    return out[:K] + out[K : 2 * K] + out[2 * K :]


def coeff_stack(coeff):
    a, b, c = split3(coeff)
    return jnp.concatenate([a, b, c, a, b, a], axis=0)


def value_stack(a, b, c):
    return jnp.concatenate([a, a, a, b, b, c], axis=0)


def combine(coeffs, values):
    return lax.dot_general(coeffs, values, (((0,), (0,)), ((), ())), preferred_element_type=F32)


def gram_part(first, second):
    one = jnp.concatenate(split3(jnp.concatenate([first, second], axis=1)), axis=0)
    two = jnp.concatenate(split3(jnp.concatenate([second, first], axis=1)), axis=0)
    out = lax.dot_general(one, two, (((1,), (1,)), ((), ())), preferred_element_type=F32)
    rows = out[:K] + out[K : 2 * K] + out[2 * K :]
    total = 0.5 * (rows[:, :K] + rows[:, K : 2 * K] + rows[:, 2 * K :])
    return jnp.concatenate([total[8 * a : 8 * a + 8] for a in range(4)], axis=1)


def unpacked(packed):
    return jnp.concatenate([packed[:, K * a : K * a + K] for a in range(4)], axis=0)


def solve(matrix, rhs):
    work = jnp.concatenate([matrix, rhs], axis=1)
    row_no = lax.broadcasted_iota(jnp.int32, work.shape, 0)
    for k in range(K):
        col = work[:, k : k + 1]
        row = work[k : k + 1, :]
        scaled = row * (1.0 / work[k : k + 1, k : k + 1])
        work = jnp.where(row_no == k, scaled, work - col * scaled)
    return work[:, K:]


def kernel(
    schur_hbm, precond_hbm, rs_ref, match_ref, x_out, r_out,
    a_mat, m_mat, rperm, msrc, rp, lz, mnext, u, full, hold, vsrc, perm_src, cont, vz,
    ar_src, ar_x, ar_y, ar_z, parts,
    mat_sem, init_sem, near_sem, gat_sem, ar_sem, send_sem,
):
    sx, sy = lax.axis_index("sx"), lax.axis_index("sy")
    nsx = NY * NZL
    y, zl = sx // NZL, sx % NZL
    zh, xc = sy // NXC, sy % NXC
    oz = 1 - zh
    z = zh * NZL + zl
    left, right = (sx + nsx - 1) % nsx, (sx + 1) % nsx
    far = oz * NXC + xc

    def x_peer(d):
        return (sx, zh * NXC + (xc + d) % NXC)

    def y_peer(d):
        return (((y + d) % NY) * NZL + zl, sy)

    def z_peer(d):
        other = (z + d) % NZ
        return (y * NZL + other % NZL, (other // NZL) * NXC + xc)

    peers = (
        [x_peer(d) for d in range(1, NXC)] + [y_peer(d) for d in range(1, NY)] + [z_peer(d) for d in range(1, NZ)]
        + [(left, sy), (right, sy), (left, far), (right, far)]
    )
    barrier = pltpu.get_barrier_semaphore()
    for peer in peers:
        pl.semaphore_signal(barrier, inc=1, device_id=peer, device_id_type=MESH)
    load_m = pltpu.make_async_copy(precond_hbm, m_mat, mat_sem.at[0])
    load_a = pltpu.make_async_copy(schur_hbm, a_mat, mat_sem.at[1])
    load_m.start()
    load_a.start()

    def copy(src, dst, recv, peer):
        return pltpu.make_async_remote_copy(
            src_ref=src, dst_ref=dst, send_sem=send_sem, recv_sem=recv, device_id=peer, device_id_type=MESH
        )

    sent = []

    def send(src, dst, recv, peer):
        copy(src, dst, recv, peer).start()
        sent.append(src)

    def arrived(ref, recv):
        copy(ref, ref, recv, (sx, sy)).wait_recv()

    spots = lax.broadcasted_iota(jnp.int32, (FB, FB), 0)
    mine = (spots == match_ref[...]).astype(BF16)
    rperm[...] = moved(rs_ref[...], mine, 0)
    msrc[...] = jnp.broadcast_to(match_ref[...], msrc.shape)
    pl.semaphore_wait(barrier, len(peers))

    send(rperm, rp.at[zh], init_sem.at[0], (left, sy))
    send(rperm, rp.at[zh], init_sem.at[0], (left, far))
    send(rs_ref, lz, init_sem.at[1], (sx, far))
    send(msrc, mnext, init_sem.at[2], (left, sy))

    def gather(slabs, recv):
        for d in range(1, NXC):
            send(slabs.at[xc], slabs.at[xc], recv, x_peer(d))

    def gathered(slabs, recv):
        arrived(slabs.at[pl.ds(0, NXC - 1)], recv)

    arrived(rp, init_sem.at[0])
    arrived(lz, init_sem.at[1])
    own = jnp.concatenate([rs_ref[...], rp[zh]], axis=1)
    other = jnp.concatenate([lz[...], rp[oz]], axis=1)

    def spread(no, slot, own, other, rounded):
        if rounded is not None:
            u[rounded, xc, zh] = own.astype(BF16)
            u[rounded, xc, oz] = other.astype(BF16)
            gather(u.at[rounded], gat_sem.at[4 + rounded])
        full[no, xc, zh] = own
        full[no, xc, oz] = other
        gather(full.at[no], gat_sem.at[no])

    spread(0, xc, own, other, 0)
    arrived(mnext, init_sem.at[2])
    following = (spots == mnext[0:1, :]).astype(BF16)

    def product(matrix, vector):
        total = jnp.zeros((K, 2 * FB), F32)
        for b in range(NXC * NZH):
            total += lax.dot_general(
                vector[b % NXC, b // NXC], matrix[:, 2 * FB * b : 2 * FB * (b + 1)],
                (((1,), (1,)), ((), ())), preferred_element_type=F32,
            )
        return total

    def tell(no, value):
        vsrc[no] = value
        send(vsrc.at[no], vz.at[no], near_sem.at[no, 0], (sx, far))
        perm_src[no, 0] = moved(value[:, FB:], following, 1)
        send(perm_src.at[no, 0], cont.at[no, zh, 0], near_sem.at[no, 1], (right, sy))
        send(perm_src.at[no, 0], cont.at[no, zh, 0], near_sem.at[no, 1], (right, far))
        perm_src[no, 1] = moved(value[:, :FB], mine, 0)
        send(perm_src.at[no, 1], cont.at[no, zh, 1], near_sem.at[no, 1], (left, sy))
        send(perm_src.at[no, 1], cont.at[no, zh, 1], near_sem.at[no, 1], (left, far))

    def assembled(no):
        arrived(vz.at[no], near_sem.at[no, 0])
        arrived(cont.at[no], near_sem.at[no, 1])
        own = vsrc[no] + jnp.concatenate([cont[no, zh, 0], cont[no, zh, 1]], axis=1)
        other = vz[no] + jnp.concatenate([cont[no, oz, 0], cont[no, oz, 1]], axis=1)
        return own, other

    def phase(no, step, value, slots, peer, me, n):
        slots[no, me] = value
        for d in range(1, n):
            send(slots.at[no, me], slots.at[no, me], ar_sem.at[no, step], peer(d))

    def phase_end(no, step, slots, n):
        arrived(slots.at[no, pl.ds(0, n - 1)], ar_sem.at[no, step])
        total = slots[no, 0]
        for i in range(1, n):
            total = total + slots[no, i]
        return total

    def reduce_x(no, value):
        phase(no, 0, value, ar_x, x_peer, xc, NXC)

    def reduce_y(no):
        phase(no, 1, phase_end(no, 0, ar_x, NXC), ar_y, y_peer, y, NY)

    def reduce_z(no):
        phase(no, 2, phase_end(no, 1, ar_y, NY), ar_z, z_peer, z, NZ)

    def reduced(no):
        return phase_end(no, 2, ar_z, NZ)

    def split_full(no):
        def body(i, carry):
            for j in range(NZH):
                for p, piece in enumerate(split3(full[no, i, j])):
                    parts[i, j, p] = piece
            return carry

        lax.fori_loop(0, NXC, body, 0)

    def stacked(i, j):
        return value_stack(parts[i, j, 0], parts[i, j, 1], parts[i, j, 2])

    load_m.wait()
    gathered(u.at[0], gat_sem.at[4])
    value = product(m_mat, u.at[0])
    tell(0, value)
    gamma_part = gram_part(own, value)
    own, other = assembled(0)
    spread(1, xc, own, other, 1)

    load_a.wait()
    gathered(u.at[1], gat_sem.at[5])
    value = product(a_mat, u.at[1])
    delta_part = gram_part(own, value)
    reduce_x(0, jnp.concatenate([gamma_part, delta_part], axis=0))
    tell(1, value)
    reduce_y(0)
    own, other = assembled(1)
    spread(2, xc, own, other, None)
    reduce_z(0)
    gathered(full.at[0], gat_sem.at[0])
    gathered(full.at[1], gat_sem.at[1])
    gathered(full.at[2], gat_sem.at[2])
    split_full(2)
    grams = reduced(0)
    gamma = unpacked(grams[:8])
    alpha = coeff_stack(solve(unpacked(grams[8:]), gamma))

    def residual_block(i, carry):
        for j in range(NZH):
            new = full[0, i, j] - combine(alpha, stacked(i, j))
            hold[0, i, j] = new
            u[2, i, j] = new.astype(BF16)
        return carry

    lax.fori_loop(0, NXC, residual_block, 0)

    value = product(m_mat, u.at[2])
    own_r = hold[0, xc, zh]
    blank = jnp.zeros((8, FB), F32)
    reduce_x(1, jnp.concatenate([gram_part(own_r, value), blank], axis=0))
    tell(2, value)
    reduce_y(1)
    own, other = assembled(2)
    spread(3, xc, own, other, None)
    reduce_z(1)
    eye = (lax.broadcasted_iota(jnp.int32, (K, K), 0) == lax.broadcasted_iota(jnp.int32, (K, K), 1)).astype(F32)
    ginv = coeff_stack(solve(gamma, eye))
    first_x = combine(alpha, value_stack(*split3(full[1, xc, zh][:, :FB])))
    split_full(1)

    def scaled_block(i, carry):
        for j in range(NZH):
            scaled = combine(ginv, stacked(i, j))
            for p, piece in enumerate(split3(scaled)):
                parts[i, j, p] = piece
        return carry

    lax.fori_loop(0, NXC, scaled_block, 0)
    gathered(full.at[3], gat_sem.at[3])
    gnew = unpacked(reduced(1)[:8])
    gnews = coeff_stack(gnew)

    def search_block(i, carry):
        for j in range(NZH):
            new = full[3, i, j] + combine(gnews, stacked(i, j))
            hold[1, i, j] = new
            u[3, i, j] = new.astype(BF16)
        return carry

    lax.fori_loop(0, NXC, search_block, 0)

    value = product(a_mat, u.at[3])
    own_p = hold[1, xc, zh]
    reduce_x(2, jnp.concatenate([gram_part(own_p, value), blank], axis=0))
    perm_src[3, 0] = moved(value[:, FB:], following, 1)
    send(perm_src.at[3, 0], cont.at[3, 0, 0], near_sem.at[3, 1], (right, sy))
    reduce_y(2)
    reduce_z(2)
    arrived(cont.at[3, 0, 0], near_sem.at[3, 1])
    q_stack = value_stack(*split3(value[:, :FB] + cont[3, 0, 0]))
    p_stack = value_stack(*split3(own_p[:, :FB]))
    alpha = coeff_stack(solve(unpacked(reduced(2)[:8]), gnew))
    x_out[...] = first_x + combine(alpha, p_stack)
    r_out[...] = own_r[:, :FB] - combine(alpha, q_stack)
    for src in sent:
        copy(src, src, init_sem.at[0], (sx, sy)).wait_send()


def shards(schur, precond, right_side, matching):
    block = jax.ShapeDtypeStruct((K, FB), F32)
    any_space = pl.BlockSpec(memory_space=pl.ANY)
    vmem = pl.BlockSpec(memory_space=pltpu.VMEM)
    rows, cols = schur.shape[1:]
    wide = 2 * FB
    x, r = pl.pallas_call(
        kernel,
        out_shape=(block, block),
        in_specs=[any_space, any_space, vmem, vmem],
        out_specs=(vmem, vmem),
        scratch_shapes=[
            pltpu.VMEM((rows, cols), BF16), pltpu.VMEM((rows, cols), BF16),
            pltpu.VMEM((K, FB), F32), pltpu.VMEM((8, FB), jnp.int32),
            pltpu.VMEM((NZH, K, FB), F32), pltpu.VMEM((K, FB), F32), pltpu.VMEM((8, FB), jnp.int32),
            pltpu.VMEM((4, NXC, NZH, K, wide), BF16),
            pltpu.VMEM((4, NXC, NZH, K, wide), F32), pltpu.VMEM((2, NXC, NZH, K, wide), F32),
            pltpu.VMEM((3, K, wide), F32), pltpu.VMEM((4, 2, K, FB), F32),
            pltpu.VMEM((4, NZH, 2, K, FB), F32), pltpu.VMEM((3, K, wide), F32),
            pltpu.VMEM((8, FB), F32),
            pltpu.VMEM((3, NXC, 16, FB), F32), pltpu.VMEM((3, NY, 16, FB), F32), pltpu.VMEM((3, NZ, 16, FB), F32),
            pltpu.VMEM((NXC, NZH, 3, K, wide), BF16),
            pltpu.SemaphoreType.DMA((2,)), pltpu.SemaphoreType.DMA((3,)), pltpu.SemaphoreType.DMA((4, 2)),
            pltpu.SemaphoreType.DMA((6,)), pltpu.SemaphoreType.DMA((3, 3)), pltpu.SemaphoreType.DMA,
        ],
        compiler_params=pltpu.CompilerParams(collective_id=0, has_side_effects=True, vmem_limit_bytes=40 * 2**20),
        name="schwarz_cg",
    )(schur[0], precond[0], right_side[0], matching)
    return x[None], r[None]


def solution(mesh):
    in_specs = (P("sx", "sy", None), P("sx", "sy", None), P("sx", None, "sy"), P("sx", "sy"))
    out_specs = (P("sx", None, "sy"), P("sx", None, "sy"))
    return jax.shard_map(shards, mesh=mesh, in_specs=in_specs, out_specs=out_specs, check_vma=False)
```

```python
import functools

import jax
import jax.numpy as jnp
from jax import lax
from jax.experimental import pallas as pl
from jax.experimental.pallas import tpu as pltpu
from jax.sharding import PartitionSpec as P

F32, BF16 = jnp.float32, jnp.bfloat16
MESH = pl.DeviceIdType.MESH
NY, NZL, NZH, NXC = 8, 6, 2, 8
NZ = NZL * NZH
K, FB = 32, 128


def split3(value):
    high = value.astype(BF16)
    rest = value - high.astype(F32)
    middle = rest.astype(BF16)
    low = (rest - middle.astype(F32)).astype(BF16)
    return high, middle, low


def moved(value, onehot, dim):
    parts = jnp.concatenate(split3(value), axis=0)
    out = lax.dot_general(parts, onehot, (((1,), (dim,)), ((), ())), preferred_element_type=F32)
    return out[:K] + out[K : 2 * K] + out[2 * K :]


def coeff_stack(coeff):
    a, b, c = split3(coeff)
    return jnp.concatenate([a, b, c, a, b, a], axis=0)


def value_stack(a, b, c):
    return jnp.concatenate([a, a, a, b, b, c], axis=0)


def combine(coeffs, values):
    return lax.dot_general(coeffs, values, (((0,), (0,)), ((), ())), preferred_element_type=F32)


def gram_part(first, second):
    one = jnp.concatenate(split3(jnp.concatenate([first, second], axis=1)), axis=0)
    two = jnp.concatenate(split3(jnp.concatenate([second, first], axis=1)), axis=0)
    out = lax.dot_general(one, two, (((1,), (1,)), ((), ())), preferred_element_type=F32)
    rows = out[:K] + out[K : 2 * K] + out[2 * K :]
    total = 0.5 * (rows[:, :K] + rows[:, K : 2 * K] + rows[:, 2 * K :])
    return jnp.concatenate([total[8 * a : 8 * a + 8] for a in range(4)], axis=1)


def unpacked(packed):
    return jnp.concatenate([packed[:, K * a : K * a + K] for a in range(4)], axis=0)


PANEL = 8


def solve(matrix, rhs):
    work = jnp.concatenate([matrix, rhs], axis=1)
    row_no = lax.broadcasted_iota(jnp.int32, work.shape, 0)
    for first in range(0, K, PANEL):
        cols = [jnp.broadcast_to(work[:, k : k + 1], work.shape) for k in range(first, first + PANEL)]
        for q in range(PANEL):
            k = first + q
            inverse = 1.0 / cols[q][k : k + 1]
            row = work[k : k + 1] * inverse
            work = jnp.where(row_no == k, row, work - cols[q] * row)
            for p in range(q + 1, PANEL):
                factor = cols[p][k : k + 1] * inverse
                cols[p] = jnp.where(row_no == k, factor, cols[p] - cols[q] * factor)
    return work[:, K:]


def kernel(
    schur_hbm, precond_hbm, rs_hbm, match_hbm, x_out, r_out,
    rs_ref, match_ref, a_rows, m_rows, a_mat, m_mat, rperm, msrc, rp, lz, mnext, u, full, hold, vsrc, perm_src, cont, vz,
    ar_x, ar_y, ar_z, parts,
    mat_sem, init_sem, near_sem, gat_sem, ar_sem, send_sem,
):
    sx, sy = lax.axis_index("sx"), lax.axis_index("sy")
    nsx = NY * NZL
    y, zl = sx // NZL, sx % NZL
    zh, xc = sy // NXC, sy % NXC
    oz = 1 - zh
    z = zh * NZL + zl
    left, right = (sx + nsx - 1) % nsx, (sx + 1) % nsx
    far = oz * NXC + xc

    def x_peer(d):
        return (sx, zh * NXC + (xc + d) % NXC)

    def y_peer(d):
        return (((y + d) % NY) * NZL + zl, sy)

    def z_peer(d):
        other = (z + d) % NZ
        return (y * NZL + other % NZL, (other // NZL) * NXC + xc)

    peers = (
        [x_peer(d) for d in range(1, NXC)] + [y_peer(d) for d in range(1, NY)] + [z_peer(d) for d in range(1, NZ)]
        + [(left, sy), (right, sy), (left, far), (right, far)]
    )
    barrier = pltpu.get_barrier_semaphore()
    for peer in peers:
        pl.semaphore_signal(barrier, inc=1, device_id=peer, device_id_type=MESH)
    load_m = pltpu.make_async_copy(precond_hbm, m_rows, mat_sem.at[0])
    load_a = pltpu.make_async_copy(schur_hbm, a_rows, mat_sem.at[1])
    load_r = pltpu.make_async_copy(rs_hbm, rs_ref, mat_sem.at[2])
    load_p = pltpu.make_async_copy(match_hbm, match_ref, mat_sem.at[3])
    load_r.start()
    load_p.start()
    load_m.start()
    load_a.start()

    def copy(src, dst, recv, peer):
        return pltpu.make_async_remote_copy(
            src_ref=src, dst_ref=dst, send_sem=send_sem, recv_sem=recv, device_id=peer, device_id_type=MESH
        )

    sent = []

    def send(src, dst, recv, peer):
        copy(src, dst, recv, peer).start()
        sent.append(src)

    def arrived(ref, recv):
        copy(ref, ref, recv, (sx, sy)).wait_recv()

    load_p.wait()
    load_r.wait()
    spots = lax.broadcasted_iota(jnp.int32, (FB, FB), 0)
    mine = (spots == match_ref[...]).astype(BF16)
    rperm[...] = moved(rs_ref[...], mine, 0)
    msrc[...] = jnp.broadcast_to(match_ref[...], msrc.shape)
    pl.semaphore_wait(barrier, len(peers))

    send(rperm, rp.at[zh], init_sem.at[0], (left, sy))
    send(rperm, rp.at[zh], init_sem.at[0], (left, far))
    send(rs_ref, lz, init_sem.at[1], (sx, far))
    send(msrc, mnext, init_sem.at[2], (left, sy))

    def transposed(source, target):
        for b in range(NXC * NZH):
            target[2 * FB * b : 2 * FB * (b + 1), :] = source[:, 2 * FB * b : 2 * FB * (b + 1)].T

    load_m.wait()
    transposed(m_rows, m_mat)
    load_a.wait()
    transposed(a_rows, a_mat)

    def gather(slabs, recv):
        for d in range(1, NXC):
            send(slabs.at[xc], slabs.at[xc], recv, x_peer(d))

    def gathered(slabs, recv):
        arrived(slabs.at[pl.ds(0, NXC - 1)], recv)

    arrived(rp, init_sem.at[0])
    arrived(lz, init_sem.at[1])
    own = jnp.concatenate([rs_ref[...], rp[zh]], axis=1)
    other = jnp.concatenate([lz[...], rp[oz]], axis=1)

    def spread(no, own, other, rounded):
        if rounded is not None:
            u[rounded, xc, zh] = own.astype(BF16)
            u[rounded, xc, oz] = other.astype(BF16)
            gather(u.at[rounded], gat_sem.at[4 + rounded])
        full[no, xc, zh] = own
        full[no, xc, oz] = other
        gather(full.at[no], gat_sem.at[no])

    spread(0, own, other, 0)
    arrived(mnext, init_sem.at[2])
    following = (spots == mnext[0:1, :]).astype(BF16)

    def product(matrix, vector):
        total = jnp.zeros((K, 2 * FB), F32)
        for b in range(NXC * NZH):
            total += lax.dot_general(
                vector[b % NXC, b // NXC], matrix[2 * FB * b : 2 * FB * (b + 1), :],
                (((1,), (0,)), ((), ())), preferred_element_type=F32,
            )
        return total

    def tell_partner(no, value):
        vsrc[no] = value
        send(vsrc.at[no], vz.at[no], near_sem.at[no, 0], (sx, far))

    def tell(no, value):
        perm_src[no, 0] = moved(value[:, FB:], following, 1)
        send(perm_src.at[no, 0], cont.at[no, zh, 0], near_sem.at[no, 1], (right, sy))
        send(perm_src.at[no, 0], cont.at[no, zh, 0], near_sem.at[no, 1], (right, far))
        perm_src[no, 1] = moved(value[:, :FB], mine, 0)
        send(perm_src.at[no, 1], cont.at[no, zh, 1], near_sem.at[no, 1], (left, sy))
        send(perm_src.at[no, 1], cont.at[no, zh, 1], near_sem.at[no, 1], (left, far))

    def assembled(no):
        arrived(vz.at[no], near_sem.at[no, 0])
        arrived(cont.at[no], near_sem.at[no, 1])
        own = vsrc[no] + jnp.concatenate([cont[no, zh, 0], cont[no, zh, 1]], axis=1)
        other = vz[no] + jnp.concatenate([cont[no, oz, 0], cont[no, oz, 1]], axis=1)
        return own, other

    def phase(no, step, value, slots, peer, me, n):
        slots[no, me] = value
        for d in range(1, n):
            send(slots.at[no, me], slots.at[no, me], ar_sem.at[no, step], peer(d))

    def phase_end(no, step, slots, n):
        arrived(slots.at[no, pl.ds(0, n - 1)], ar_sem.at[no, step])
        total = slots[no, 0]
        for i in range(1, n):
            total = total + slots[no, i]
        return total

    def reduce_x(no, value):
        phase(no, 0, value, ar_x, x_peer, xc, NXC)

    def reduce_y(no):
        phase(no, 1, phase_end(no, 0, ar_x, NXC), ar_y, y_peer, y, NY)

    def reduce_z(no):
        phase(no, 2, phase_end(no, 1, ar_y, NY), ar_z, z_peer, z, NZ)

    def reduced(no):
        return phase_end(no, 2, ar_z, NZ)

    def split_full(no):
        def body(i, carry):
            for j in range(NZH):
                for p, piece in enumerate(split3(full[no, i, j])):
                    parts[i, j, p] = piece
            return carry

        for i in range(NXC):
            body(i, 0)

    def stacked(i, j):
        return value_stack(parts[i, j, 0], parts[i, j, 1], parts[i, j, 2])

    gathered(u.at[0], gat_sem.at[4])
    value = product(m_mat, u.at[0])
    tell_partner(0, value)
    tell(0, value)
    reduce_x(0, gram_part(own, value))
    own, other = assembled(0)
    spread(1, own, other, 1)
    reduce_y(0)

    gathered(u.at[1], gat_sem.at[5])
    value = product(a_mat, u.at[1])
    tell_partner(1, value)
    reduce_x(1, gram_part(own, value))
    tell(1, value)
    reduce_z(0)
    reduce_y(1)
    own, other = assembled(1)
    spread(2, own, other, None)
    reduce_z(1)
    gathered(full.at[0], gat_sem.at[0])
    gathered(full.at[1], gat_sem.at[1])
    gathered(full.at[2], gat_sem.at[2])
    split_full(2)
    gamma = unpacked(reduced(0))
    alpha = coeff_stack(solve(unpacked(reduced(1)), gamma))

    def residual_block(i, carry):
        for j in range(NZH):
            new = full[0, i, j] - combine(alpha, stacked(i, j))
            hold[0, i, j] = new
            u[2, i, j] = new.astype(BF16)
        return carry

    for i in range(NXC):
        residual_block(i, 0)

    value = product(m_mat, u.at[2])
    own_r = hold[0, xc, zh]
    tell_partner(2, value)
    reduce_x(2, gram_part(own_r, value))
    tell(2, value)
    reduce_y(2)
    own, other = assembled(2)
    spread(3, own, other, None)
    reduce_z(2)
    eye = (lax.broadcasted_iota(jnp.int32, (K, K), 0) == lax.broadcasted_iota(jnp.int32, (K, K), 1)).astype(F32)
    ginv = coeff_stack(solve(gamma, eye))
    first_x = combine(alpha, value_stack(*split3(full[1, xc, zh][:, :FB])))
    split_full(1)

    def scaled_block(i, carry):
        for j in range(NZH):
            scaled = combine(ginv, stacked(i, j))
            for p, piece in enumerate(split3(scaled)):
                parts[i, j, p] = piece
        return carry

    for i in range(NXC):
        scaled_block(i, 0)
    gathered(full.at[3], gat_sem.at[3])
    gnew = unpacked(reduced(2))
    gnews = coeff_stack(gnew)

    def search_block(i, carry):
        for j in range(NZH):
            new = full[3, i, j] + combine(gnews, stacked(i, j))
            hold[1, i, j] = new
            u[3, i, j] = new.astype(BF16)
        return carry

    for i in range(NXC):
        search_block(i, 0)

    value = product(a_mat, u.at[3])
    own_p = hold[1, xc, zh]
    reduce_x(3, gram_part(own_p, value))
    perm_src[3, 0] = moved(value[:, FB:], following, 1)
    send(perm_src.at[3, 0], cont.at[3, 0, 0], near_sem.at[3, 1], (right, sy))
    reduce_y(3)
    reduce_z(3)
    arrived(cont.at[3, 0, 0], near_sem.at[3, 1])
    q_stack = value_stack(*split3(value[:, :FB] + cont[3, 0, 0]))
    p_stack = value_stack(*split3(own_p[:, :FB]))
    alpha = coeff_stack(solve(unpacked(reduced(3)), gnew))
    x_out[...] = first_x + combine(alpha, p_stack)
    r_out[...] = own_r[:, :FB] - combine(alpha, q_stack)
    for src in sent:
        copy(src, src, init_sem.at[0], (sx, sy)).wait_send()


def shards(schur, precond, right_side, matching):
    block = jax.ShapeDtypeStruct((K, FB), F32)
    hbm = pl.BlockSpec(memory_space=pltpu.HBM)
    vmem = pl.BlockSpec(memory_space=pltpu.VMEM)
    rows, cols = schur.shape[1:]
    wide = 2 * FB
    x, r = pl.pallas_call(
        kernel,
        out_shape=(block, block),
        in_specs=[hbm, hbm, hbm, hbm],
        out_specs=(vmem, vmem),
        scratch_shapes=[
            pltpu.VMEM((K, FB), F32), pltpu.VMEM((1, FB), jnp.int32),
            pltpu.VMEM((rows, cols), BF16), pltpu.VMEM((rows, cols), BF16),
            pltpu.VMEM((cols, rows), BF16), pltpu.VMEM((cols, rows), BF16),
            pltpu.VMEM((K, FB), F32), pltpu.VMEM((8, FB), jnp.int32),
            pltpu.VMEM((NZH, K, FB), F32), pltpu.VMEM((K, FB), F32), pltpu.VMEM((8, FB), jnp.int32),
            pltpu.VMEM((4, NXC, NZH, K, wide), BF16),
            pltpu.VMEM((4, NXC, NZH, K, wide), F32), pltpu.VMEM((2, NXC, NZH, K, wide), F32),
            pltpu.VMEM((3, K, wide), F32), pltpu.VMEM((4, 2, K, FB), F32),
            pltpu.VMEM((4, NZH, 2, K, FB), F32), pltpu.VMEM((3, K, wide), F32),
            pltpu.VMEM((4, NXC, 8, FB), F32), pltpu.VMEM((4, NY, 8, FB), F32), pltpu.VMEM((4, NZ, 8, FB), F32),
            pltpu.VMEM((NXC, NZH, 3, K, wide), BF16),
            pltpu.SemaphoreType.DMA((4,)), pltpu.SemaphoreType.DMA((3,)), pltpu.SemaphoreType.DMA((4, 2)),
            pltpu.SemaphoreType.DMA((6,)), pltpu.SemaphoreType.DMA((4, 3)), pltpu.SemaphoreType.DMA,
        ],
        compiler_params=pltpu.CompilerParams(collective_id=0, has_side_effects=True, vmem_limit_bytes=64 * 2**20),
        name="schwarz_cg",
    )(schur[0], precond[0], right_side[0], matching)
    return x[None], r[None]


def solution(mesh):
    in_specs = (P("sx", "sy", None), P("sx", "sy", None), P("sx", None, "sy"), P("sx", "sy"))
    out_specs = (P("sx", None, "sy"), P("sx", None, "sy"))
    return jax.shard_map(shards, mesh=mesh, in_specs=in_specs, out_specs=out_specs, check_vma=False)
```

```python
import functools

import jax
import jax.numpy as jnp
from jax import lax
from jax.experimental import pallas as pl
from jax.experimental.pallas import tpu as pltpu
from jax.sharding import PartitionSpec as P

F32, BF16 = jnp.float32, jnp.bfloat16
MESH = pl.DeviceIdType.MESH
NY, NZL, NZH, NXC = 8, 6, 2, 8
NZ = NZL * NZH
K, FB = 32, 128


def far_first(n):
    return sorted(range(1, n), key=lambda d: -min(d, n - d))


def split3(value):
    high = value.astype(BF16)
    rest = value - high.astype(F32)
    middle = rest.astype(BF16)
    low = (rest - middle.astype(F32)).astype(BF16)
    return high, middle, low


def moved(value, onehot, dim):
    parts = jnp.concatenate(split3(value), axis=0)
    out = lax.dot_general(parts, onehot, (((1,), (dim,)), ((), ())), preferred_element_type=F32)
    return out[:K] + out[K : 2 * K] + out[2 * K :]


def coeff_stack(coeff):
    a, b, c = split3(coeff)
    return jnp.concatenate([a, b, c, a, b, a], axis=0)


def value_stack(a, b, c):
    return jnp.concatenate([a, a, a, b, b, c], axis=0)


def combine(coeffs, values):
    return lax.dot_general(coeffs, values, (((0,), (0,)), ((), ())), preferred_element_type=F32)


def gram_part(first, second):
    one = jnp.concatenate(split3(jnp.concatenate([first, second], axis=1)), axis=0)
    two = jnp.concatenate(split3(jnp.concatenate([second, first], axis=1)), axis=0)
    out = lax.dot_general(one, two, (((1,), (1,)), ((), ())), preferred_element_type=F32)
    rows = out[:K] + out[K : 2 * K] + out[2 * K :]
    total = 0.5 * (rows[:, :K] + rows[:, K : 2 * K] + rows[:, 2 * K :])
    return jnp.concatenate([total[8 * a : 8 * a + 8] for a in range(4)], axis=1)


def unpacked(packed):
    return jnp.concatenate([packed[:, K * a : K * a + K] for a in range(4)], axis=0)


PANEL = 8


def solve(matrix, rhs):
    work = jnp.concatenate([matrix, rhs], axis=1)
    row_no = lax.broadcasted_iota(jnp.int32, work.shape, 0)
    for first in range(0, K, PANEL):
        cols = [jnp.broadcast_to(work[:, k : k + 1], work.shape) for k in range(first, first + PANEL)]
        for q in range(PANEL):
            k = first + q
            inverse = 1.0 / cols[q][k : k + 1]
            row = work[k : k + 1] * inverse
            work = jnp.where(row_no == k, row, work - cols[q] * row)
            for p in range(q + 1, PANEL):
                factor = cols[p][k : k + 1] * inverse
                cols[p] = jnp.where(row_no == k, factor, cols[p] - cols[q] * factor)
    return work[:, K:]


def kernel(
    schur_hbm, precond_hbm, rs_hbm, match_hbm, out,
    rs_ref, match_ref, a_rows, m_rows, a_mat, m_mat, rperm, msrc, rp, lz, mnext, u, full, hold, vsrc, perm_src, cont, vz,
    ar_x, ar_y, ar_z, parts,
    mat_sem, init_sem, near_sem, gat_sem, ar_sem, send_sem,
):
    sx, sy = lax.axis_index("sx"), lax.axis_index("sy")
    nsx = NY * NZL
    y, zl = sx // NZL, sx % NZL
    zh, xc = sy // NXC, sy % NXC
    oz = 1 - zh
    z = zh * NZL + zl
    left, right = (sx + nsx - 1) % nsx, (sx + 1) % nsx
    far = oz * NXC + xc

    def x_peer(d):
        return (sx, zh * NXC + (xc + d) % NXC)

    def y_peer(d):
        return (((y + d) % NY) * NZL + zl, sy)

    def z_peer(d):
        other = (z + d) % NZ
        return (y * NZL + other % NZL, (other // NZL) * NXC + xc)

    peers = (
        [x_peer(d) for d in range(1, NXC)] + [y_peer(d) for d in range(1, NY)] + [z_peer(d) for d in range(1, NZ)]
        + [(left, sy), (right, sy), (left, far), (right, far)]
    )
    barrier = pltpu.get_barrier_semaphore()
    for peer in peers:
        pl.semaphore_signal(barrier, inc=1, device_id=peer, device_id_type=MESH)
    load_m = pltpu.make_async_copy(precond_hbm, m_rows, mat_sem.at[0])
    load_a = pltpu.make_async_copy(schur_hbm, a_rows, mat_sem.at[1])
    load_r = pltpu.make_async_copy(rs_hbm, rs_ref, mat_sem.at[2])
    load_p = pltpu.make_async_copy(match_hbm, match_ref, mat_sem.at[3])
    load_r.start()
    load_p.start()
    load_m.start()
    load_a.start()

    def copy(src, dst, recv, peer):
        return pltpu.make_async_remote_copy(
            src_ref=src, dst_ref=dst, send_sem=send_sem, recv_sem=recv, device_id=peer, device_id_type=MESH
        )

    sent = []

    def send(src, dst, recv, peer):
        copy(src, dst, recv, peer).start()
        sent.append(src)

    def arrived(ref, recv):
        copy(ref, ref, recv, (sx, sy)).wait_recv()

    load_p.wait()
    load_r.wait()
    spots = lax.broadcasted_iota(jnp.int32, (FB, FB), 0)
    mine = (spots == match_ref[...]).astype(BF16)
    rperm[...] = moved(rs_ref[...], mine, 0)
    msrc[...] = jnp.broadcast_to(match_ref[...], msrc.shape)
    pl.semaphore_wait(barrier, len(peers))

    send(rperm, rp.at[zh], init_sem.at[0], (left, sy))
    send(rperm, rp.at[zh], init_sem.at[0], (left, far))
    send(rs_ref, lz, init_sem.at[1], (sx, far))
    send(msrc, mnext, init_sem.at[2], (left, sy))

    def transposed(source, target):
        for b in range(NXC * NZH):
            target[2 * FB * b : 2 * FB * (b + 1), :] = source[:, 2 * FB * b : 2 * FB * (b + 1)].T

    load_m.wait()
    transposed(m_rows, m_mat)
    load_a.wait()
    transposed(a_rows, a_mat)

    def gather(slabs, recv):
        for d in far_first(NXC):
            send(slabs.at[xc], slabs.at[xc], recv, x_peer(d))

    def gathered(slabs, recv):
        arrived(slabs.at[pl.ds(0, NXC - 1)], recv)

    arrived(rp, init_sem.at[0])
    arrived(lz, init_sem.at[1])
    own = jnp.concatenate([rs_ref[...], rp[zh]], axis=1)
    other = jnp.concatenate([lz[...], rp[oz]], axis=1)

    def spread(no, own, other, rounded):
        if rounded is not None:
            u[rounded, xc, zh] = own.astype(BF16)
            u[rounded, xc, oz] = other.astype(BF16)
            gather(u.at[rounded], gat_sem.at[4 + rounded])
        full[no, xc, zh] = own
        full[no, xc, oz] = other
        if rounded is None:
            gather(full.at[no], gat_sem.at[no])

    spread(0, own, other, 0)
    arrived(mnext, init_sem.at[2])
    following = (spots == mnext[0:1, :]).astype(BF16)

    def product(matrix, vector):
        total = jnp.zeros((K, 2 * FB), F32)
        for b in range(NXC * NZH):
            total += lax.dot_general(
                vector[b % NXC, b // NXC], matrix[2 * FB * b : 2 * FB * (b + 1), :],
                (((1,), (0,)), ((), ())), preferred_element_type=F32,
            )
        return total

    def tell_partner(no, value):
        vsrc[no] = value
        send(vsrc.at[no], vz.at[no], near_sem.at[no, 0], (sx, far))

    def tell(no, value):
        perm_src[no, 0] = moved(value[:, FB:], following, 1)
        send(perm_src.at[no, 0], cont.at[no, zh, 0], near_sem.at[no, 1], (right, sy))
        send(perm_src.at[no, 0], cont.at[no, zh, 0], near_sem.at[no, 1], (right, far))
        perm_src[no, 1] = moved(value[:, :FB], mine, 0)
        send(perm_src.at[no, 1], cont.at[no, zh, 1], near_sem.at[no, 1], (left, sy))
        send(perm_src.at[no, 1], cont.at[no, zh, 1], near_sem.at[no, 1], (left, far))

    def assembled(no):
        arrived(vz.at[no], near_sem.at[no, 0])
        arrived(cont.at[no], near_sem.at[no, 1])
        own = vsrc[no] + jnp.concatenate([cont[no, zh, 0], cont[no, zh, 1]], axis=1)
        other = vz[no] + jnp.concatenate([cont[no, oz, 0], cont[no, oz, 1]], axis=1)
        return own, other

    def phase(no, step, value, slots, peer, me, n):
        slots[no, me] = value
        for d in far_first(n):
            send(slots.at[no, me], slots.at[no, me], ar_sem.at[no, step], peer(d))

    def phase_end(no, step, slots, n):
        arrived(slots.at[no, pl.ds(0, n - 1)], ar_sem.at[no, step])
        total = slots[no, 0]
        for i in range(1, n):
            total = total + slots[no, i]
        return total

    def reduce_x(no, value):
        phase(no, 0, value, ar_x, x_peer, xc, NXC)

    def reduce_y(no):
        phase(no, 1, phase_end(no, 0, ar_x, NXC), ar_y, y_peer, y, NY)

    def reduce_z(no):
        phase(no, 2, phase_end(no, 1, ar_y, NY), ar_z, z_peer, z, NZ)

    def reduced(no):
        return phase_end(no, 2, ar_z, NZ)

    def split_full(no):
        def body(i, carry):
            for j in range(NZH):
                for p, piece in enumerate(split3(full[no, i, j])):
                    parts[i, j, p] = piece
            return carry

        for i in range(NXC):
            body(i, 0)

    def stacked(i, j):
        return value_stack(parts[i, j, 0], parts[i, j, 1], parts[i, j, 2])

    gathered(u.at[0], gat_sem.at[4])
    gather(full.at[0], gat_sem.at[0])
    value = product(m_mat, u.at[0])
    tell_partner(0, value)
    tell(0, value)
    reduce_x(0, gram_part(own, value))
    own, other = assembled(0)
    spread(1, own, other, 1)
    reduce_y(0)

    gathered(u.at[1], gat_sem.at[5])
    value = product(a_mat, u.at[1])
    tell_partner(1, value)
    reduce_x(1, gram_part(own, value))
    tell(1, value)
    reduce_z(0)
    reduce_y(1)
    own, other = assembled(1)
    spread(2, own, other, None)
    reduce_z(1)
    gathered(full.at[0], gat_sem.at[0])
    gathered(full.at[2], gat_sem.at[2])
    gather(full.at[1], gat_sem.at[1])
    split_full(2)
    gamma = unpacked(reduced(0))
    alpha = coeff_stack(solve(unpacked(reduced(1)), gamma))

    def residual_block(i, carry):
        for j in range(NZH):
            new = full[0, i, j] - combine(alpha, stacked(i, j))
            hold[0, i, j] = new
            u[2, i, j] = new.astype(BF16)
        return carry

    for i in range(NXC):
        residual_block(i, 0)

    value = product(m_mat, u.at[2])
    own_r = hold[0, xc, zh]
    tell_partner(2, value)
    reduce_x(2, gram_part(own_r, value))
    tell(2, value)
    reduce_y(2)
    own, other = assembled(2)
    spread(3, own, other, None)
    reduce_z(2)
    eye = (lax.broadcasted_iota(jnp.int32, (K, K), 0) == lax.broadcasted_iota(jnp.int32, (K, K), 1)).astype(F32)
    ginv = coeff_stack(solve(gamma, eye))
    first_x = combine(alpha, value_stack(*split3(full[1, xc, zh][:, :FB])))
    gathered(full.at[1], gat_sem.at[1])
    split_full(1)

    def scaled_block(i, carry):
        for j in range(NZH):
            scaled = combine(ginv, stacked(i, j))
            for p, piece in enumerate(split3(scaled)):
                parts[i, j, p] = piece
        return carry

    for i in range(NXC):
        scaled_block(i, 0)
    gathered(full.at[3], gat_sem.at[3])
    gnew = unpacked(reduced(2))
    gnews = coeff_stack(gnew)

    def search_block(i, carry):
        for j in range(NZH):
            new = full[3, i, j] + combine(gnews, stacked(i, j))
            hold[1, i, j] = new
            u[3, i, j] = new.astype(BF16)
        return carry

    for i in range(NXC):
        search_block(i, 0)

    value = product(a_mat, u.at[3])
    own_p = hold[1, xc, zh]
    reduce_x(3, gram_part(own_p, value))
    perm_src[3, 0] = moved(value[:, FB:], following, 1)
    send(perm_src.at[3, 0], cont.at[3, 0, 0], near_sem.at[3, 1], (right, sy))
    reduce_y(3)
    reduce_z(3)
    arrived(cont.at[3, 0, 0], near_sem.at[3, 1])
    q_stack = value_stack(*split3(value[:, :FB] + cont[3, 0, 0]))
    p_stack = value_stack(*split3(own_p[:, :FB]))
    alpha = coeff_stack(solve(unpacked(reduced(3)), gnew))
    out[0] = first_x + combine(alpha, p_stack)
    out[1] = own_r[:, :FB] - combine(alpha, q_stack)
    for src in sent:
        copy(src, src, init_sem.at[0], (sx, sy)).wait_send()


def shards(schur, precond, right_side, matching):
    hbm = pl.BlockSpec(memory_space=pltpu.HBM)
    vmem = pl.BlockSpec(memory_space=pltpu.VMEM)
    rows, cols = schur.shape[1:]
    wide = 2 * FB
    out = pl.pallas_call(
        kernel,
        out_shape=jax.ShapeDtypeStruct((2, K, FB), F32),
        in_specs=[hbm, hbm, hbm, hbm],
        out_specs=vmem,
        scratch_shapes=[
            pltpu.VMEM((K, FB), F32), pltpu.VMEM((1, FB), jnp.int32),
            pltpu.VMEM((rows, cols), BF16), pltpu.VMEM((rows, cols), BF16),
            pltpu.VMEM((cols, rows), BF16), pltpu.VMEM((cols, rows), BF16),
            pltpu.VMEM((K, FB), F32), pltpu.VMEM((8, FB), jnp.int32),
            pltpu.VMEM((NZH, K, FB), F32), pltpu.VMEM((K, FB), F32), pltpu.VMEM((8, FB), jnp.int32),
            pltpu.VMEM((4, NXC, NZH, K, wide), BF16),
            pltpu.VMEM((4, NXC, NZH, K, wide), F32), pltpu.VMEM((2, NXC, NZH, K, wide), F32),
            pltpu.VMEM((3, K, wide), F32), pltpu.VMEM((4, 2, K, FB), F32),
            pltpu.VMEM((4, NZH, 2, K, FB), F32), pltpu.VMEM((3, K, wide), F32),
            pltpu.VMEM((4, NXC, 8, FB), F32), pltpu.VMEM((4, NY, 8, FB), F32), pltpu.VMEM((4, NZ, 8, FB), F32),
            pltpu.VMEM((NXC, NZH, 3, K, wide), BF16),
            pltpu.SemaphoreType.DMA((4,)), pltpu.SemaphoreType.DMA((3,)), pltpu.SemaphoreType.DMA((4, 2)),
            pltpu.SemaphoreType.DMA((6,)), pltpu.SemaphoreType.DMA((4, 3)), pltpu.SemaphoreType.DMA,
        ],
        compiler_params=pltpu.CompilerParams(collective_id=0, has_side_effects=True, vmem_limit_bytes=64 * 2**20),
        name="schwarz_cg",
    )(schur[0], precond[0], right_side[0], matching)
    return out[0:1], out[1:2]


def solution(mesh):
    in_specs = (P("sx", "sy", None), P("sx", "sy", None), P("sx", None, "sy"), P("sx", "sy"))
    out_specs = (P("sx", None, "sy"), P("sx", None, "sy"))
    return jax.shard_map(shards, mesh=mesh, in_specs=in_specs, out_specs=out_specs, check_vma=False)
```
